32 devices in a mesh: group: 2 (over x), mp: 16 (over z, y, core).
Axes of the slice: x: 2, y: 2, z: 4, core: 2. Of those that a mesh axis runs over, the one named last changes fastest.
Arguments:
- tokens: bfloat16 [4096, 8192], P(('group', 'mp')), parts along dimension 0, may hold values from -6 to 6
- norm_gain: float32 [8192], replicated, may hold values from 0.5 to 2
- query_tiles: bfloat16 [32768, 2048], P('mp'), may hold values from -0.0625 to 0.0625
- key_weight_tiles: bfloat16 [32768, 256], P('mp'), may hold values from -0.0625 to 0.0625
- value_weight_tiles: bfloat16 [32768, 256], P('mp'), may hold values from -0.0625 to 0.0625
- output_tiles: bfloat16 [32768, 2048], P('mp'), may hold values from -0.25 to 0.25
- visits: int32 [8, 512], P('group'), parts along dimension 0, may hold values from 0 to 31, as said below
- lengths: int32 [8], P('group'), parts along dimension 0, may hold values from 128 to 512, as said below
Outputs:
- attended: bfloat16 [4096, 8192], P(('group', 'mp')), parts along dimension 0
The draws below stay inside these ranges and needn't reach their ends.
There are 2 independent parts, one for each index of `group`. The reference program is written for one: setup_inputs(seed, part) draws one part's arguments, and reference() takes and returns one part's arrays. A program takes and returns all parts, laid end to end along the dimension named above; an argument that names none is the same for every part. Nothing has to cross between parts.
Inputs may be any that keep to these rules, and one draw needn't show every extreme that they name: `visits`: each row starts at 0, rises by 0 or 1 from one token to the next, and ends at 31. `lengths`: one timeline of each part has all 512 tokens real.
All inputs are finite; a program needn't handle non-finite values.
Results may differ from the reference program's by a relative error of at most 0.012.
Values may be sent and summed in bfloat16 or wider, within the bound.
A program may use at most 320 MiB of HBM per device.

```python
import math
import jax
import jax.numpy as jnp
from jax import lax

MODEL_WIDTH = 8192
QUERY_HEADS = 64
KEY_VALUE_HEADS = 8
HEAD_SIZE = 128
PART_TIMELINES = 4
TIMELINE_TOKENS = 512
TOKENS = 2048
QCOL = 2048
KCOL = 256
N_MP = 16


def draw_visits(key, part):
    key = jax.random.fold_in(key, 11)
    row_keys = jax.random.split(key, PART_TIMELINES)
    orders = jax.vmap(lambda row_key: jax.random.permutation(row_key, TIMELINE_TOKENS - 1))(row_keys)
    starts = (orders < TIMELINE_TOKENS // 16 - 1).astype(jnp.int32)
    starts = jnp.concatenate([jnp.zeros((PART_TIMELINES, 1), jnp.int32), starts], axis=1)
    return jnp.cumsum(starts, axis=1).astype(jnp.int32)


def draw_lengths(key, part):
    key = jax.random.fold_in(key, 12)
    drawn = jax.random.randint(key, (PART_TIMELINES,), TIMELINE_TOKENS // 4, TIMELINE_TOKENS + 1)
    chosen = jax.random.randint(jax.random.fold_in(key, 5), (), 0, PART_TIMELINES)
    return jnp.where(jnp.arange(PART_TIMELINES) == chosen, TIMELINE_TOKENS, drawn).astype(jnp.int32)


def block_levels(key, shape, cuts, smallest, largest):
    gain, own = 1.0, jax.random.fold_in(key, 6)
    for position, parts in cuts:
        steps = jnp.exp(jax.random.uniform(jax.random.fold_in(own, position), (parts,), jnp.float32, smallest / len(cuts), largest / len(cuts)))
        gain = gain * jnp.repeat(steps, shape[position] // parts).reshape([-1 if axis == position else 1 for axis in range(len(shape))])
    return gain


def scatter_about(own_key, shape, scale, most, cuts=(), kind=jnp.bfloat16):
    entries = jax.random.normal(own_key, shape, jnp.float32) * scale
    if len(cuts) > 0:
        entries = block_levels(own_key, shape, cuts, -0.22, 0.18) * entries
    return jnp.clip(entries, min=-most, max=most).astype(kind)


def setup_inputs(seed: int = 0, part: int = 0) -> dict:
    keys = jax.random.split(jax.random.key(seed), 9)
    part_splits = jax.random.split(jax.random.fold_in(keys[8], part), 9)
    tokens = scatter_about(part_splits[0], (TOKENS, MODEL_WIDTH), 1.0, 6.0, ((0, 16),))
    norm_gain = jnp.clip(jnp.exp(jax.random.uniform(keys[1], (MODEL_WIDTH,), jnp.float32, math.log(0.5), math.log(2.0))), 0.5, 2.0)
    query_tiles = scatter_about(keys[2], (N_MP * (MODEL_WIDTH // PART_TIMELINES), QCOL), MODEL_WIDTH ** -0.5, 0.0625, ((0, 16),))
    key_weight_tiles = scatter_about(keys[3], (N_MP * (MODEL_WIDTH // PART_TIMELINES), KCOL), MODEL_WIDTH ** -0.5, 0.0625, ((0, 16),))
    value_weight_tiles = scatter_about(keys[4], (N_MP * (MODEL_WIDTH // PART_TIMELINES), KCOL), MODEL_WIDTH ** -0.5, 0.0625, ((0, 16),))
    output_tiles = scatter_about(keys[5], (N_MP * QCOL, MODEL_WIDTH // PART_TIMELINES), (QUERY_HEADS * HEAD_SIZE // 16) ** -0.5, 0.25, ((0, 16),))
    visits = draw_visits(jax.random.fold_in(jax.random.fold_in(keys[8], part), 71), part)
    lengths = draw_lengths(jax.random.fold_in(jax.random.fold_in(keys[8], part), 71), part)
    return dict(tokens=tokens, norm_gain=norm_gain, query_tiles=query_tiles, key_weight_tiles=key_weight_tiles, value_weight_tiles=value_weight_tiles, output_tiles=output_tiles, visits=visits, lengths=lengths)


def rotary_embedding(value_rows):
    positions = jnp.arange(value_rows.shape[0], dtype=jnp.float32)
    half_width = value_rows.shape[-1] // 2
    inverse = jnp.power(500000.0, -jnp.arange(half_width, dtype=jnp.float32) * 2.0 / value_rows.shape[-1])
    angles = positions[:, None, None] * inverse[None, None, :]
    cosine = jnp.cos(angles)
    sine = jnp.sin(angles)
    first = value_rows[..., :half_width]
    second = value_rows[..., half_width:]
    return jnp.concatenate([first * cosine - second * sine, second * cosine + first * sine], axis=-1)

def reference(tokens, norm_gain, query_tiles, key_weight_tiles, value_weight_tiles, output_tiles, visits, lengths):
    group_total = N_MP // PART_TIMELINES
    part_rows = MODEL_WIDTH // PART_TIMELINES
    query_weight = query_tiles.reshape(PART_TIMELINES, group_total, part_rows, -1).transpose(0, 2, 1, 3).reshape(MODEL_WIDTH, QUERY_HEADS * HEAD_SIZE)
    key_matrix = key_weight_tiles.reshape(PART_TIMELINES, group_total, part_rows, -1).transpose(0, 2, 1, 3).reshape(MODEL_WIDTH, KEY_VALUE_HEADS * HEAD_SIZE)
    value_matrix = value_weight_tiles.reshape(PART_TIMELINES, group_total, part_rows, -1).transpose(0, 2, 1, 3).reshape(MODEL_WIDTH, KEY_VALUE_HEADS * HEAD_SIZE)
    output_weight = output_tiles.reshape(PART_TIMELINES, group_total, -1, part_rows).transpose(1, 2, 0, 3).reshape(QUERY_HEADS * HEAD_SIZE, MODEL_WIDTH)
    widened = tokens.astype(jnp.float32)
    normed = (widened * lax.rsqrt(lax.optimization_barrier(jnp.mean(widened * widened, axis=1, keepdims=True)) + 1e-05) * norm_gain.astype(jnp.float32)).astype(jnp.bfloat16)
    positions = jnp.arange(TIMELINE_TOKENS, dtype=jnp.int32)
    results = []
    for timeline in range(PART_TIMELINES):
        visit_block = normed[timeline * TIMELINE_TOKENS:(timeline + 1) * TIMELINE_TOKENS]
        query_vectors = jnp.dot(visit_block, query_weight, preferred_element_type=jnp.float32).reshape(TIMELINE_TOKENS, QUERY_HEADS, HEAD_SIZE)
        query_vectors = (rotary_embedding(query_vectors) * HEAD_SIZE ** (-0.5)).astype(jnp.bfloat16).reshape(TIMELINE_TOKENS, KEY_VALUE_HEADS, QUERY_HEADS // KEY_VALUE_HEADS, HEAD_SIZE)
        key_rows = rotary_embedding(jnp.dot(visit_block, key_matrix, preferred_element_type=jnp.float32).reshape(TIMELINE_TOKENS, KEY_VALUE_HEADS, HEAD_SIZE)).astype(jnp.bfloat16)
        value_rows = jnp.dot(visit_block, value_matrix, preferred_element_type=jnp.float32).astype(jnp.bfloat16).reshape(TIMELINE_TOKENS, KEY_VALUE_HEADS, HEAD_SIZE)
        visit_row = visits[timeline]
        allowed = (visit_row[None, :] <= visit_row[:, None]) & (positions[None, :] < lengths[timeline])
        scores = jnp.einsum('qhgd,khd->hgqk', query_vectors.astype(jnp.float32), key_rows.astype(jnp.float32))
        raw_weights = jnp.where(allowed, jnp.exp(scores), 0.0)
        probs = (raw_weights / lax.optimization_barrier(jnp.sum(raw_weights, axis=-1, keepdims=True))).astype(jnp.bfloat16)
        heads = jnp.einsum('hgqk,khd->qhgd', probs.astype(jnp.float32), value_rows.astype(jnp.float32)).astype(jnp.bfloat16).reshape(TIMELINE_TOKENS, QUERY_HEADS * HEAD_SIZE)
        results.append(jnp.dot(heads, output_weight, preferred_element_type=jnp.float32).astype(jnp.bfloat16))
    return jnp.concatenate(results, axis=0)
```

```python
import jax
import jax.numpy as jnp
from jax import lax
from jax.sharding import PartitionSpec as P

KEY_VALUE_HEADS = 8
HEAD_SIZE = 128
PART_TIMELINES = 4


def partner_2(value, axis, bit):
    mask = 2**bit
    pairs = [(source, source ^ mask) for source in range(lax.axis_size(axis))]
    return lax.ppermute(value, axis, pairs)


def upper_half(device_index, bit_number):
    return device_index // (1 << bit_number) % 2 == 1


def joined(current, partner, partner_first, axis_number):
    lower = jnp.where(partner_first, partner, current)
    higher = jnp.where(partner_first, current, partner)
    return jnp.concatenate([lower, higher], axis=axis_number)


def butterfly(pieces, device_index, bit_count, mover):
    count = pieces.shape[0]
    rest = pieces.shape[1:]
    for bit_number in range(bit_count):
        split = pieces.reshape((count >> bit_number + 1, 2, 1 << bit_number) + rest)
        upper_side = upper_half(device_index, bit_number)
        kept = jnp.where(upper_side, split[:, 1], split[:, 0])
        given = jnp.where(upper_side, split[:, 0], split[:, 1])
        arrived = mover(given, bit_number)
        lower = jnp.where(upper_side, arrived, kept)
        higher = jnp.where(upper_side, kept, arrived)
        pieces = jnp.stack([lower, higher], axis=1).reshape((count,) + rest)
    return pieces


def rotary_embedding(value_rows):
    positions = jnp.arange(value_rows.shape[0], dtype=jnp.float32)
    half_width = value_rows.shape[-1] // 2
    inverse = jnp.power(
        500000.0, -jnp.arange(half_width, dtype=jnp.float32) * 2.0 / value_rows.shape[-1]
    )
    angles = positions[:, None, None] * inverse[None, None, :]
    cosine = jnp.cos(angles)
    sine = jnp.sin(angles)
    first = value_rows[..., :half_width]
    second = value_rows[..., half_width:]
    return jnp.concatenate(
        [first * cosine - second * sine, second * cosine + first * sine], axis=-1
    )


def gathered_weight_shards(
    tokens,
    norm_gain,
    query_tiles,
    key_weight_tiles,
    value_weight_tiles,
    output_tiles,
    visits,
    lengths,
):
    query_head_groups = lax.axis_size("mp") // PART_TIMELINES
    group_bits = query_head_groups.bit_length() - 1
    timeline_bits = PART_TIMELINES.bit_length() - 1
    device_index = lax.axis_index("mp")
    timeline = device_index // query_head_groups
    widened = tokens.astype(jnp.float32)
    normed = (
        widened * lax.rsqrt(jnp.mean(widened * widened, axis=1, keepdims=True) + 1e-05) * norm_gain
    ).astype(jnp.bfloat16)
    gathered = normed
    for bit_number in range(group_bits):
        partner = partner_2(gathered, "mp", bit_number)
        gathered = joined(gathered, partner, upper_half(device_index, bit_number), 0)
    query_weight = query_tiles
    for section_number in range(timeline_bits):
        bit_number = group_bits + section_number
        partner = partner_2(query_weight, "mp", bit_number)
        query_weight = joined(query_weight, partner, upper_half(device_index, bit_number), 0)
    head_repeats = max(1, query_head_groups // KEY_VALUE_HEADS)
    repeat_bits = head_repeats.bit_length() - 1
    stacked = jnp.stack([key_weight_tiles, value_weight_tiles])
    roster = [(group_bits + section_number, 1) for section_number in range(timeline_bits)]
    roster = roster + [(section_number, 2) for section_number in range(repeat_bits)]
    for bit_number, axis_number in roster:
        partner = partner_2(stacked, "mp", bit_number)
        stacked = joined(stacked, partner, upper_half(device_index, bit_number), axis_number)
    projected = jnp.einsum("td,sdc->stc", gathered, stacked, preferred_element_type=jnp.float32)
    timeline_rows = gathered.shape[0]
    key_rows = rotary_embedding(projected[0].reshape(timeline_rows, -1, HEAD_SIZE)).astype(
        jnp.bfloat16
    )
    value_rows = projected[1].astype(jnp.bfloat16).reshape(timeline_rows, -1, HEAD_SIZE)
    local_kv = key_rows.shape[1]
    query_vectors = jnp.dot(gathered, query_weight, preferred_element_type=jnp.float32).reshape(
        timeline_rows, -1, HEAD_SIZE
    )
    local_heads = query_vectors.shape[1]
    query_vectors = (
        (rotary_embedding(query_vectors) * HEAD_SIZE ** (-0.5))
        .astype(jnp.bfloat16)
        .reshape(timeline_rows, local_kv, local_heads // local_kv, HEAD_SIZE)
    )
    visit_row = lax.dynamic_index_in_dim(visits, timeline, 0, keepdims=False)
    real_count = lax.dynamic_index_in_dim(lengths, timeline, 0, keepdims=False)
    positions = jnp.arange(timeline_rows, dtype=jnp.int32)
    allowed = (visit_row[None, :] <= visit_row[:, None]) & (positions[None, :] < real_count)
    scores = jnp.einsum(
        "qhgd,khd->hgqk", query_vectors, key_rows, preferred_element_type=jnp.float32
    )
    raw_weights = jnp.where(allowed, jnp.exp(scores), 0.0)
    probs = (raw_weights / jnp.sum(raw_weights, axis=-1, keepdims=True)).astype(jnp.bfloat16)
    heads = (
        jnp.einsum("hgqk,khd->qhgd", probs, value_rows, preferred_element_type=jnp.float32)
        .astype(jnp.bfloat16)
        .reshape(timeline_rows, -1)
    )
    owned = tokens.shape[0]
    all_heads = heads
    for bit_number in range(group_bits):
        partner = partner_2(all_heads, "mp", bit_number)
        all_heads = joined(all_heads, partner, upper_half(device_index, bit_number), 1)
    tile_rows = output_tiles.shape[0]
    blocks = output_tiles.reshape(tile_rows, query_head_groups, -1).transpose(1, 0, 2)

    def move_blocks(given, bit_number):
        return partner_2(given, "mp", bit_number)

    blocks = butterfly(blocks, device_index, group_bits, move_blocks)
    narrow = blocks.shape[2]
    column_weight = blocks.reshape(query_head_groups * tile_rows, narrow)
    for section_number in range(timeline_bits):
        bit_number = group_bits + section_number
        partner = partner_2(column_weight, "mp", bit_number)
        column_weight = joined(column_weight, partner, upper_half(device_index, bit_number), 1)
    finished = jnp.dot(all_heads, column_weight, preferred_element_type=jnp.float32).astype(
        jnp.bfloat16
    )
    outgoing = finished.reshape(query_head_groups, owned, PART_TIMELINES * narrow)

    def move_rows(given, bit_number):
        return partner_2(given, "mp", bit_number)

    incoming = butterfly(outgoing, device_index, group_bits, move_rows)
    incoming = incoming.reshape(query_head_groups, owned, PART_TIMELINES, narrow).transpose(
        1, 2, 0, 3
    )
    return incoming.reshape(owned, PART_TIMELINES * query_head_groups * narrow)


def hop(value, pairs):
    mp = lax.axis_size("mp")
    span = mp // PART_TIMELINES
    full = [(a * span + s, b * span + s) for a, b in pairs for s in range(span)]
    return lax.ppermute(value, "mp", full)


def rotated(value, cosine, sine):
    half = HEAD_SIZE // 2
    first, second = value[..., :half], value[..., half:]
    return jnp.concatenate(
        [first * cosine - second * sine, second * cosine + first * sine], axis=-1
    )


def attention(queries, keys, values, allowed):
    scores = jnp.einsum("qgd,kd->gqk", queries, keys, preferred_element_type=jnp.float32)
    raw = jnp.where(allowed, jnp.exp(scores), 0.0)
    probs = (raw / jnp.sum(raw, axis=-1, keepdims=True)).astype(jnp.bfloat16)
    heads = jnp.einsum("gqk,kd->qgd", probs, values, preferred_element_type=jnp.float32)
    return heads.astype(jnp.bfloat16).reshape(queries.shape[0], -1)


PIECES = 2


def resident_weight_shards(
    tokens,
    norm_gain,
    query_tiles,
    key_weight_tiles,
    value_weight_tiles,
    output_tiles,
    visits,
    lengths,
):
    ring = PART_TIMELINES
    device_index = lax.axis_index("mp")
    plane = device_index // 4
    place = device_index % 4
    owned, width = tokens.shape
    depth = width // ring
    rows = 4 * owned
    widened = tokens.astype(jnp.float32)
    normed = (
        widened * lax.rsqrt(jnp.mean(widened * widened, axis=1, keepdims=True) + 1e-05) * norm_gain
    ).astype(jnp.bfloat16)

    slots = []
    for r in range(ring):
        start = (plane + r) % ring * depth
        block = lax.dynamic_slice_in_dim(normed, start, depth, 1)
        if r > 0:
            block = hop(block, [(z, (z + r) % ring) for z in range(ring)])
        pair = jnp.stack([block, partner_2(block, "mp", 1)])
        other = partner_2(pair, "mp", 0)
        slots.append(jnp.stack([pair[0], other[0], pair[1], other[1]]).reshape(rows, depth))

    order = [place ^ j for j in range(4)]
    positions = jnp.concatenate(
        [o * owned + jnp.arange(owned, dtype=jnp.int32) for o in order]
    )
    visit_row = lax.dynamic_index_in_dim(visits, plane, 0, keepdims=False)
    visit_row = jnp.concatenate(
        [lax.dynamic_slice_in_dim(visit_row, o * owned, owned, 0) for o in order]
    )
    real_count = lax.dynamic_index_in_dim(lengths, plane, 0, keepdims=False)
    allowed = (visit_row[None, :] <= visit_row[:, None]) & (positions[None, :] < real_count)
    half = HEAD_SIZE // 2
    inverse = jnp.power(500000.0, -jnp.arange(half, dtype=jnp.float32) * 2.0 / HEAD_SIZE)
    angles = positions.astype(jnp.float32)[:, None] * inverse[None, :]
    cosine, sine = jnp.cos(angles), jnp.sin(angles)

    local_kv = key_weight_tiles.shape[1] // HEAD_SIZE
    columns = query_tiles.shape[1]
    repeats = PIECES // local_kv
    step = columns // PIECES
    right = [(z, z + 1) for z in range(ring - 1)]
    left = [(z + 1, z) for z in range(ring - 1)]
    totals = [None] * ring
    keys = values = None
    for piece in range(PIECES):
        has_kv = piece % repeats == 0
        weight = query_tiles[:, piece * step : (piece + 1) * step]
        if has_kv:
            kv = piece // repeats
            span = slice(kv * HEAD_SIZE, (kv + 1) * HEAD_SIZE)
            weight = jnp.concatenate(
                [weight, key_weight_tiles[:, span], value_weight_tiles[:, span]], axis=1
            )

        def part(r):
            return jnp.dot(slots[r], weight, preferred_element_type=jnp.float32)

        going_right, going_left = part(1), part(3)
        middle = None
        for k in range(1, ring):
            arrived_right = hop(going_right.astype(jnp.bfloat16), right[:k])
            arrived_left = hop(going_left.astype(jnp.bfloat16), left[ring - 1 - k :])
            if k < ring - 1:
                going_right = part(k + 1) + arrived_right.astype(jnp.float32)
                going_left = part(ring - 1 - k) + arrived_left.astype(jnp.float32)
        summed = part(0) + arrived_right.astype(jnp.float32) + arrived_left.astype(jnp.float32)
        if has_kv:
            keys = rotated(summed[:, step : step + HEAD_SIZE], cosine, sine).astype(jnp.bfloat16)
            values = summed[:, step + HEAD_SIZE :].astype(jnp.bfloat16)
        queries = rotated(
            summed[:, :step].reshape(rows, -1, HEAD_SIZE), cosine[:, None], sine[:, None]
        )
        queries = (queries * HEAD_SIZE ** (-0.5)).astype(jnp.bfloat16)
        own = attention(queries, keys, values, allowed)
        from_left, from_right = [own], [own]
        for k in range(1, ring):
            from_left.append(hop(from_left[-1], right[k - 1 :]))
            from_right.append(hop(from_right[-1], left[: ring - k]))
        out_rows = output_tiles[piece * step : (piece + 1) * step]
        for r in range(ring):
            block = own if r == 0 else jnp.where(plane >= r, from_left[r], from_right[ring - r])
            product = jnp.dot(block, out_rows, preferred_element_type=jnp.float32)
            totals[r] = product if totals[r] is None else totals[r] + product

    out = jnp.zeros((owned, width), jnp.bfloat16)
    for r in (0, 2, 3, 1):
        four = totals[r].reshape(4, owned, depth)
        away = jnp.stack([four[1], four[3]]).astype(jnp.bfloat16)
        arrived = partner_2(away, "mp", 0).astype(jnp.float32)
        far = (four[2] + arrived[1]).astype(jnp.bfloat16)
        near = four[0] + arrived[0] + partner_2(far, "mp", 1).astype(jnp.float32)
        block = near.astype(jnp.bfloat16)
        if r > 0:
            block = hop(block, [(z, (z - r) % ring) for z in range(ring)])
        out = lax.dynamic_update_slice_in_dim(out, block, (plane + r) % ring * depth, 1)
    return out


def solution(mesh):
    resident = mesh.shape["mp"] == 4 * PART_TIMELINES
    return jax.shard_map(
        resident_weight_shards if resident else gathered_weight_shards,
        mesh=mesh,
        in_specs=(
            P(("group", "mp"), None),
            P(),
            P("mp", None),
            P("mp", None),
            P("mp", None),
            P("mp", None),
            P("group", None),
            P("group"),
        ),
        out_specs=P(("group", "mp"), None),
        check_vma=False,
    )
```

```python
import jax
import jax.numpy as jnp
from jax import lax
from jax.sharding import PartitionSpec as P

KEY_VALUE_HEADS = 8
HEAD_SIZE = 128
PART_TIMELINES = 4


def partner_2(value, axis, bit):
    mask = 2**bit
    pairs = [(source, source ^ mask) for source in range(lax.axis_size(axis))]
    return lax.ppermute(value, axis, pairs)


def upper_half(device_index, bit_number):
    return device_index // (1 << bit_number) % 2 == 1


def joined(current, partner, partner_first, axis_number):
    lower = jnp.where(partner_first, partner, current)
    higher = jnp.where(partner_first, current, partner)
    return jnp.concatenate([lower, higher], axis=axis_number)


def butterfly(pieces, device_index, bit_count, mover):
    count = pieces.shape[0]
    rest = pieces.shape[1:]
    for bit_number in range(bit_count):
        split = pieces.reshape((count >> bit_number + 1, 2, 1 << bit_number) + rest)
        upper_side = upper_half(device_index, bit_number)
        kept = jnp.where(upper_side, split[:, 1], split[:, 0])
        given = jnp.where(upper_side, split[:, 0], split[:, 1])
        arrived = mover(given, bit_number)
        lower = jnp.where(upper_side, arrived, kept)
        higher = jnp.where(upper_side, kept, arrived)
        pieces = jnp.stack([lower, higher], axis=1).reshape((count,) + rest)
    return pieces


def rotary_embedding(value_rows):
    positions = jnp.arange(value_rows.shape[0], dtype=jnp.float32)
    half_width = value_rows.shape[-1] // 2
    inverse = jnp.power(
        500000.0, -jnp.arange(half_width, dtype=jnp.float32) * 2.0 / value_rows.shape[-1]
    )
    angles = positions[:, None, None] * inverse[None, None, :]
    cosine = jnp.cos(angles)
    sine = jnp.sin(angles)
    first = value_rows[..., :half_width]
    second = value_rows[..., half_width:]
    return jnp.concatenate(
        [first * cosine - second * sine, second * cosine + first * sine], axis=-1
    )


def gathered_weight_shards(
    tokens,
    norm_gain,
    query_tiles,
    key_weight_tiles,
    value_weight_tiles,
    output_tiles,
    visits,
    lengths,
):
    query_head_groups = lax.axis_size("mp") // PART_TIMELINES
    group_bits = query_head_groups.bit_length() - 1
    timeline_bits = PART_TIMELINES.bit_length() - 1
    device_index = lax.axis_index("mp")
    timeline = device_index // query_head_groups
    widened = tokens.astype(jnp.float32)
    normed = (
        widened * lax.rsqrt(jnp.mean(widened * widened, axis=1, keepdims=True) + 1e-05) * norm_gain
    ).astype(jnp.bfloat16)
    gathered = normed
    for bit_number in range(group_bits):
        partner = partner_2(gathered, "mp", bit_number)
        gathered = joined(gathered, partner, upper_half(device_index, bit_number), 0)
    query_weight = query_tiles
    for section_number in range(timeline_bits):
        bit_number = group_bits + section_number
        partner = partner_2(query_weight, "mp", bit_number)
        query_weight = joined(query_weight, partner, upper_half(device_index, bit_number), 0)
    head_repeats = max(1, query_head_groups // KEY_VALUE_HEADS)
    repeat_bits = head_repeats.bit_length() - 1
    stacked = jnp.stack([key_weight_tiles, value_weight_tiles])
    roster = [(group_bits + section_number, 1) for section_number in range(timeline_bits)]
    roster = roster + [(section_number, 2) for section_number in range(repeat_bits)]
    for bit_number, axis_number in roster:
        partner = partner_2(stacked, "mp", bit_number)
        stacked = joined(stacked, partner, upper_half(device_index, bit_number), axis_number)
    projected = jnp.einsum("td,sdc->stc", gathered, stacked, preferred_element_type=jnp.float32)
    timeline_rows = gathered.shape[0]
    key_rows = rotary_embedding(projected[0].reshape(timeline_rows, -1, HEAD_SIZE)).astype(
        jnp.bfloat16
    )
    value_rows = projected[1].astype(jnp.bfloat16).reshape(timeline_rows, -1, HEAD_SIZE)
    local_kv = key_rows.shape[1]
    query_vectors = jnp.dot(gathered, query_weight, preferred_element_type=jnp.float32).reshape(
        timeline_rows, -1, HEAD_SIZE
    )
    local_heads = query_vectors.shape[1]
    query_vectors = (
        (rotary_embedding(query_vectors) * HEAD_SIZE ** (-0.5))
        .astype(jnp.bfloat16)
        .reshape(timeline_rows, local_kv, local_heads // local_kv, HEAD_SIZE)
    )
    visit_row = lax.dynamic_index_in_dim(visits, timeline, 0, keepdims=False)
    real_count = lax.dynamic_index_in_dim(lengths, timeline, 0, keepdims=False)
    positions = jnp.arange(timeline_rows, dtype=jnp.int32)
    allowed = (visit_row[None, :] <= visit_row[:, None]) & (positions[None, :] < real_count)
    scores = jnp.einsum(
        "qhgd,khd->hgqk", query_vectors, key_rows, preferred_element_type=jnp.float32
    )
    raw_weights = jnp.where(allowed, jnp.exp(scores), 0.0)
    probs = (raw_weights / jnp.sum(raw_weights, axis=-1, keepdims=True)).astype(jnp.bfloat16)
    heads = (
        jnp.einsum("hgqk,khd->qhgd", probs, value_rows, preferred_element_type=jnp.float32)
        .astype(jnp.bfloat16)
        .reshape(timeline_rows, -1)
    )
    owned = tokens.shape[0]
    all_heads = heads
    for bit_number in range(group_bits):
        partner = partner_2(all_heads, "mp", bit_number)
        all_heads = joined(all_heads, partner, upper_half(device_index, bit_number), 1)
    tile_rows = output_tiles.shape[0]
    blocks = output_tiles.reshape(tile_rows, query_head_groups, -1).transpose(1, 0, 2)

    def move_blocks(given, bit_number):
        return partner_2(given, "mp", bit_number)

    blocks = butterfly(blocks, device_index, group_bits, move_blocks)
    narrow = blocks.shape[2]
    column_weight = blocks.reshape(query_head_groups * tile_rows, narrow)
    for section_number in range(timeline_bits):
        bit_number = group_bits + section_number
        partner = partner_2(column_weight, "mp", bit_number)
        column_weight = joined(column_weight, partner, upper_half(device_index, bit_number), 1)
    finished = jnp.dot(all_heads, column_weight, preferred_element_type=jnp.float32).astype(
        jnp.bfloat16
    )
    outgoing = finished.reshape(query_head_groups, owned, PART_TIMELINES * narrow)

    def move_rows(given, bit_number):
        return partner_2(given, "mp", bit_number)

    incoming = butterfly(outgoing, device_index, group_bits, move_rows)
    incoming = incoming.reshape(query_head_groups, owned, PART_TIMELINES, narrow).transpose(
        1, 2, 0, 3
    )
    return incoming.reshape(owned, PART_TIMELINES * query_head_groups * narrow)


def hop(value, pairs):
    mp = lax.axis_size("mp")
    span = mp // PART_TIMELINES
    full = [(a * span + s, b * span + s) for a, b in pairs for s in range(span)]
    return lax.ppermute(value, "mp", full)


def rotated(value, cosine, sine):
    half = HEAD_SIZE // 2
    first, second = value[..., :half], value[..., half:]
    return jnp.concatenate(
        [first * cosine - second * sine, second * cosine + first * sine], axis=-1
    )


def attention(queries, keys, values, allowed):
    scores = jnp.einsum("qgd,kd->gqk", queries, keys, preferred_element_type=jnp.float32)
    raw = jnp.where(allowed, jnp.exp(scores), 0.0)
    probs = (raw / jnp.sum(raw, axis=-1, keepdims=True)).astype(jnp.bfloat16)
    heads = jnp.einsum("gqk,kd->qgd", probs, values, preferred_element_type=jnp.float32)
    return heads.astype(jnp.bfloat16).reshape(queries.shape[0], -1)


PIECES = 2


def resident_weight_shards(
    tokens,
    norm_gain,
    query_tiles,
    key_weight_tiles,
    value_weight_tiles,
    output_tiles,
    visits,
    lengths,
):
    ring = PART_TIMELINES
    device_index = lax.axis_index("mp")
    plane = device_index // 4
    place = device_index % 4
    owned, width = tokens.shape
    depth = width // ring
    rows = 4 * owned
    widened = tokens.astype(jnp.float32)
    normed = (
        widened * lax.rsqrt(jnp.mean(widened * widened, axis=1, keepdims=True) + 1e-05) * norm_gain
    ).astype(jnp.bfloat16)

    slots = []
    for r in range(ring):
        start = (plane + r) % ring * depth
        block = lax.dynamic_slice_in_dim(normed, start, depth, 1)
        if r > 0:
            block = hop(block, [(z, (z + r) % ring) for z in range(ring)])
        pair = jnp.stack([block, partner_2(block, "mp", 1)])
        other = partner_2(pair, "mp", 0)
        slots.append(jnp.stack([pair[0], other[0], pair[1], other[1]]).reshape(rows, depth))

    order = [place ^ j for j in range(4)]
    positions = jnp.concatenate(
        [o * owned + jnp.arange(owned, dtype=jnp.int32) for o in order]
    )
    visit_row = lax.dynamic_index_in_dim(visits, plane, 0, keepdims=False)
    visit_row = jnp.concatenate(
        [lax.dynamic_slice_in_dim(visit_row, o * owned, owned, 0) for o in order]
    )
    real_count = lax.dynamic_index_in_dim(lengths, plane, 0, keepdims=False)
    allowed = (visit_row[None, :] <= visit_row[:, None]) & (positions[None, :] < real_count)
    half = HEAD_SIZE // 2
    inverse = jnp.power(500000.0, -jnp.arange(half, dtype=jnp.float32) * 2.0 / HEAD_SIZE)
    angles = positions.astype(jnp.float32)[:, None] * inverse[None, :]
    cosine, sine = jnp.cos(angles), jnp.sin(angles)

    local_kv = key_weight_tiles.shape[1] // HEAD_SIZE
    columns = query_tiles.shape[1]
    repeats = PIECES // local_kv
    step = columns // PIECES
    right = [(z, z + 1) for z in range(ring - 1)]
    left = [(z + 1, z) for z in range(ring - 1)]
    kept = {}
    weights = []
    for piece in range(PIECES):
        weight = query_tiles[:, piece * step : (piece + 1) * step]
        if piece % repeats == 0:
            kv = piece // repeats
            span = slice(kv * HEAD_SIZE, (kv + 1) * HEAD_SIZE)
            weight = jnp.concatenate(
                [weight, key_weight_tiles[:, span], value_weight_tiles[:, span]], axis=1
            )
        weights.append(weight)

    def part(piece, r):
        product = jnp.dot(slots[r], weights[piece], preferred_element_type=jnp.float32)
        return lax.optimization_barrier(product)

    def attend(piece, summed):
        if piece % repeats == 0:
            keys = rotated(summed[:, step : step + HEAD_SIZE], cosine, sine).astype(jnp.bfloat16)
            kept[piece // repeats] = keys, summed[:, step + HEAD_SIZE :].astype(jnp.bfloat16)
        keys, values = kept[piece // repeats]
        queries = rotated(
            summed[:, :step].reshape(rows, -1, HEAD_SIZE), cosine[:, None], sine[:, None]
        )
        queries = (queries * HEAD_SIZE ** (-0.5)).astype(jnp.bfloat16)
        return attention(queries, keys, values, allowed)

    totals = [None] * ring
    arrived, summed = {}, {}
    from_left = [[] for _ in range(PIECES)]
    from_right = [[] for _ in range(PIECES)]
    hops = ring - 1
    for tick in range(1, hops * PIECES + 2 + hops):
        payloads, receivers = [], []
        attending = None
        for piece in range(PIECES):
            k = tick - hops * piece
            if 1 <= k <= hops:
                going_right, going_left = part(piece, k), part(piece, ring - k)
                if k > 1:
                    going_right += arrived[piece][0].astype(jnp.float32)
                    going_left += arrived[piece][1].astype(jnp.float32)
                payloads += [going_right.astype(jnp.bfloat16), going_left.astype(jnp.bfloat16)]
                receivers.append(("sum", piece, k))
            if k == ring:
                own = part(piece, 0)
                for value in arrived[piece]:
                    own += value.astype(jnp.float32)
                attending = piece
                payloads.insert(0, own)
            k = k - ring
            if 1 <= k <= hops:
                payloads += [from_left[piece][-1], from_right[piece][-1]]
                receivers.append(("gather", piece, k))
        payloads = list(lax.optimization_barrier(tuple(payloads)))
        if attending is not None:
            own = attend(attending, payloads.pop(0))
            from_left[attending].append(own)
            from_right[attending].append(own)
        for kind, piece, k in receivers:
            first, second = payloads.pop(0), payloads.pop(0)
            if kind == "sum":
                arrived[piece] = hop(first, right[:k]), hop(second, left[hops - k :])
            else:
                from_left[piece].append(hop(first, right[k - 1 :]))
                from_right[piece].append(hop(second, left[: ring - k]))
    for r in range(ring):
        for piece in range(PIECES):
            block = from_left[piece][0]
            if r > 0:
                block = jnp.where(
                    plane >= r, from_left[piece][r], from_right[piece][ring - r]
                )
            out_rows = output_tiles[piece * step : (piece + 1) * step]
            product = jnp.dot(block, out_rows, preferred_element_type=jnp.float32)
            totals[r] = product if totals[r] is None else totals[r] + product

    out = jnp.zeros((owned, width), jnp.bfloat16)
    for r in (0, 2, 3, 1):
        four = totals[r].reshape(4, owned, depth)
        away = jnp.stack([four[1], four[3]]).astype(jnp.bfloat16)
        arrived = partner_2(away, "mp", 0).astype(jnp.float32)
        far = (four[2] + arrived[1]).astype(jnp.bfloat16)
        near = four[0] + arrived[0] + partner_2(far, "mp", 1).astype(jnp.float32)
        block = near.astype(jnp.bfloat16)
        if r > 0:
            block = hop(block, [(z, (z - r) % ring) for z in range(ring)])
        out = lax.dynamic_update_slice_in_dim(out, block, (plane + r) % ring * depth, 1)
    return out


def solution(mesh):
    resident = mesh.shape["mp"] == 4 * PART_TIMELINES
    return jax.shard_map(
        resident_weight_shards if resident else gathered_weight_shards,
        mesh=mesh,
        in_specs=(
            P(("group", "mp"), None),
            P(),
            P("mp", None),
            P("mp", None),
            P("mp", None),
            P("mp", None),
            P("group", None),
            P("group"),
        ),
        out_specs=P(("group", "mp"), None),
        check_vma=False,
    )
```

```python
import jax
import jax.numpy as jnp
from jax import lax
from jax.sharding import PartitionSpec as P

KEY_VALUE_HEADS = 8
HEAD_SIZE = 128
PART_TIMELINES = 4


def partner_2(value, axis, bit):
    mask = 2**bit
    pairs = [(source, source ^ mask) for source in range(lax.axis_size(axis))]
    return lax.ppermute(value, axis, pairs)


def upper_half(device_index, bit_number):
    return device_index // (1 << bit_number) % 2 == 1


def joined(current, partner, partner_first, axis_number):
    lower = jnp.where(partner_first, partner, current)
    higher = jnp.where(partner_first, current, partner)
    return jnp.concatenate([lower, higher], axis=axis_number)


def butterfly(pieces, device_index, bit_count, mover):
    count = pieces.shape[0]
    rest = pieces.shape[1:]
    for bit_number in range(bit_count):
        split = pieces.reshape((count >> bit_number + 1, 2, 1 << bit_number) + rest)
        upper_side = upper_half(device_index, bit_number)
        kept = jnp.where(upper_side, split[:, 1], split[:, 0])
        given = jnp.where(upper_side, split[:, 0], split[:, 1])
        arrived = mover(given, bit_number)
        lower = jnp.where(upper_side, arrived, kept)
        higher = jnp.where(upper_side, kept, arrived)
        pieces = jnp.stack([lower, higher], axis=1).reshape((count,) + rest)
    return pieces


def rotary_embedding(value_rows):
    positions = jnp.arange(value_rows.shape[0], dtype=jnp.float32)
    half_width = value_rows.shape[-1] // 2
    inverse = jnp.power(
        500000.0, -jnp.arange(half_width, dtype=jnp.float32) * 2.0 / value_rows.shape[-1]
    )
    angles = positions[:, None, None] * inverse[None, None, :]
    cosine = jnp.cos(angles)
    sine = jnp.sin(angles)
    first = value_rows[..., :half_width]
    second = value_rows[..., half_width:]
    return jnp.concatenate(
        [first * cosine - second * sine, second * cosine + first * sine], axis=-1
    )


def gathered_weight_shards(
    tokens,
    norm_gain,
    query_tiles,
    key_weight_tiles,
    value_weight_tiles,
    output_tiles,
    visits,
    lengths,
):
    query_head_groups = lax.axis_size("mp") // PART_TIMELINES
    group_bits = query_head_groups.bit_length() - 1
    timeline_bits = PART_TIMELINES.bit_length() - 1
    device_index = lax.axis_index("mp")
    timeline = device_index // query_head_groups
    widened = tokens.astype(jnp.float32)
    normed = (
        widened * lax.rsqrt(jnp.mean(widened * widened, axis=1, keepdims=True) + 1e-05) * norm_gain
    ).astype(jnp.bfloat16)
    gathered = normed
    for bit_number in range(group_bits):
        partner = partner_2(gathered, "mp", bit_number)
        gathered = joined(gathered, partner, upper_half(device_index, bit_number), 0)
    query_weight = query_tiles
    for section_number in range(timeline_bits):
        bit_number = group_bits + section_number
        partner = partner_2(query_weight, "mp", bit_number)
        query_weight = joined(query_weight, partner, upper_half(device_index, bit_number), 0)
    head_repeats = max(1, query_head_groups // KEY_VALUE_HEADS)
    repeat_bits = head_repeats.bit_length() - 1
    stacked = jnp.stack([key_weight_tiles, value_weight_tiles])
    roster = [(group_bits + section_number, 1) for section_number in range(timeline_bits)]
    roster = roster + [(section_number, 2) for section_number in range(repeat_bits)]
    for bit_number, axis_number in roster:
        partner = partner_2(stacked, "mp", bit_number)
        stacked = joined(stacked, partner, upper_half(device_index, bit_number), axis_number)
    projected = jnp.einsum("td,sdc->stc", gathered, stacked, preferred_element_type=jnp.float32)
    timeline_rows = gathered.shape[0]
    key_rows = rotary_embedding(projected[0].reshape(timeline_rows, -1, HEAD_SIZE)).astype(
        jnp.bfloat16
    )
    value_rows = projected[1].astype(jnp.bfloat16).reshape(timeline_rows, -1, HEAD_SIZE)
    local_kv = key_rows.shape[1]
    query_vectors = jnp.dot(gathered, query_weight, preferred_element_type=jnp.float32).reshape(
        timeline_rows, -1, HEAD_SIZE
    )
    local_heads = query_vectors.shape[1]
    query_vectors = (
        (rotary_embedding(query_vectors) * HEAD_SIZE ** (-0.5))
        .astype(jnp.bfloat16)
        .reshape(timeline_rows, local_kv, local_heads // local_kv, HEAD_SIZE)
    )
    visit_row = lax.dynamic_index_in_dim(visits, timeline, 0, keepdims=False)
    real_count = lax.dynamic_index_in_dim(lengths, timeline, 0, keepdims=False)
    positions = jnp.arange(timeline_rows, dtype=jnp.int32)
    allowed = (visit_row[None, :] <= visit_row[:, None]) & (positions[None, :] < real_count)
    scores = jnp.einsum(
        "qhgd,khd->hgqk", query_vectors, key_rows, preferred_element_type=jnp.float32
    )
    raw_weights = jnp.where(allowed, jnp.exp(scores), 0.0)
    probs = (raw_weights / jnp.sum(raw_weights, axis=-1, keepdims=True)).astype(jnp.bfloat16)
    heads = (
        jnp.einsum("hgqk,khd->qhgd", probs, value_rows, preferred_element_type=jnp.float32)
        .astype(jnp.bfloat16)
        .reshape(timeline_rows, -1)
    )
    owned = tokens.shape[0]
    all_heads = heads
    for bit_number in range(group_bits):
        partner = partner_2(all_heads, "mp", bit_number)
        all_heads = joined(all_heads, partner, upper_half(device_index, bit_number), 1)
    tile_rows = output_tiles.shape[0]
    blocks = output_tiles.reshape(tile_rows, query_head_groups, -1).transpose(1, 0, 2)

    def move_blocks(given, bit_number):
        return partner_2(given, "mp", bit_number)

    blocks = butterfly(blocks, device_index, group_bits, move_blocks)
    narrow = blocks.shape[2]
    column_weight = blocks.reshape(query_head_groups * tile_rows, narrow)
    for section_number in range(timeline_bits):
        bit_number = group_bits + section_number
        partner = partner_2(column_weight, "mp", bit_number)
        column_weight = joined(column_weight, partner, upper_half(device_index, bit_number), 1)
    finished = jnp.dot(all_heads, column_weight, preferred_element_type=jnp.float32).astype(
        jnp.bfloat16
    )
    outgoing = finished.reshape(query_head_groups, owned, PART_TIMELINES * narrow)

    def move_rows(given, bit_number):
        return partner_2(given, "mp", bit_number)

    incoming = butterfly(outgoing, device_index, group_bits, move_rows)
    incoming = incoming.reshape(query_head_groups, owned, PART_TIMELINES, narrow).transpose(
        1, 2, 0, 3
    )
    return incoming.reshape(owned, PART_TIMELINES * query_head_groups * narrow)


def hop(value, pairs):
    mp = lax.axis_size("mp")
    span = mp // PART_TIMELINES
    full = [(a * span + s, b * span + s) for a, b in pairs for s in range(span)]
    return lax.ppermute(value, "mp", full)


def rotated(value, cosine, sine):
    half = HEAD_SIZE // 2
    first, second = value[..., :half], value[..., half:]
    return jnp.concatenate(
        [first * cosine - second * sine, second * cosine + first * sine], axis=-1
    )


def attention(queries, keys, values, allowed):
    scores = jnp.einsum("qgd,kd->gqk", queries, keys, preferred_element_type=jnp.float32)
    raw = jnp.where(allowed, jnp.exp(scores), 0.0)
    probs = (raw / jnp.sum(raw, axis=-1, keepdims=True)).astype(jnp.bfloat16)
    heads = jnp.einsum("gqk,kd->qgd", probs, values, preferred_element_type=jnp.float32)
    return heads.astype(jnp.bfloat16).reshape(queries.shape[0], -1)


PIECES = 2


def resident_weight_shards(
    tokens,
    norm_gain,
    query_tiles,
    key_weight_tiles,
    value_weight_tiles,
    output_tiles,
    visits,
    lengths,
):
    ring = PART_TIMELINES
    device_index = lax.axis_index("mp")
    plane = device_index // 4
    place = device_index % 4
    owned, width = tokens.shape
    depth = width // ring
    rows = 4 * owned
    widened = tokens.astype(jnp.float32)
    normed = (
        widened * lax.rsqrt(jnp.mean(widened * widened, axis=1, keepdims=True) + 1e-05) * norm_gain
    ).astype(jnp.bfloat16)

    def beside(block):
        pair = jnp.stack([block, partner_2(block, "mp", 1)])
        other = partner_2(pair, "mp", 0)
        return jnp.stack([pair[0], other[0], pair[1], other[1]]).reshape(rows, depth)

    blocks = {}
    for r in (0, 1, 3, 2):
        block = lax.dynamic_slice_in_dim(normed, (plane + r) % ring * depth, depth, 1)
        if r == 2:
            block = lax.optimization_barrier((block, blocks[1], blocks[3]))[0]
        if r > 0:
            block = hop(block, [(z, (z + r) % ring) for z in range(ring)])
        blocks[r] = block
    slots = {r: beside(blocks[r]) for r in (1, 3, 0)}

    order = [place ^ j for j in range(4)]
    positions = jnp.concatenate(
        [o * owned + jnp.arange(owned, dtype=jnp.int32) for o in order]
    )
    visit_row = lax.dynamic_index_in_dim(visits, plane, 0, keepdims=False)
    visit_row = jnp.concatenate(
        [lax.dynamic_slice_in_dim(visit_row, o * owned, owned, 0) for o in order]
    )
    real_count = lax.dynamic_index_in_dim(lengths, plane, 0, keepdims=False)
    allowed = (visit_row[None, :] <= visit_row[:, None]) & (positions[None, :] < real_count)
    half = HEAD_SIZE // 2
    inverse = jnp.power(500000.0, -jnp.arange(half, dtype=jnp.float32) * 2.0 / HEAD_SIZE)
    angles = positions.astype(jnp.float32)[:, None] * inverse[None, :]
    cosine, sine = jnp.cos(angles), jnp.sin(angles)

    local_kv = key_weight_tiles.shape[1] // HEAD_SIZE
    columns = query_tiles.shape[1]
    repeats = PIECES // local_kv
    step = columns // PIECES
    right = [(z, z + 1) for z in range(ring - 1)]
    left = [(z + 1, z) for z in range(ring - 1)]
    kept = {}
    weights = []
    for piece in range(PIECES):
        weight = query_tiles[:, piece * step : (piece + 1) * step]
        if piece % repeats == 0:
            kv = piece // repeats
            span = slice(kv * HEAD_SIZE, (kv + 1) * HEAD_SIZE)
            weight = jnp.concatenate(
                [weight, key_weight_tiles[:, span], value_weight_tiles[:, span]], axis=1
            )
        weights.append(weight)

    def part(piece, r):
        product = jnp.dot(slots[r], weights[piece], preferred_element_type=jnp.float32)
        return lax.optimization_barrier(product)

    def attend(piece, summed):
        if piece % repeats == 0:
            keys = rotated(summed[:, step : step + HEAD_SIZE], cosine, sine).astype(jnp.bfloat16)
            kept[piece // repeats] = keys, summed[:, step + HEAD_SIZE :].astype(jnp.bfloat16)
        keys, values = kept[piece // repeats]
        queries = rotated(
            summed[:, :step].reshape(rows, -1, HEAD_SIZE), cosine[:, None], sine[:, None]
        )
        queries = (queries * HEAD_SIZE ** (-0.5)).astype(jnp.bfloat16)
        return attention(queries, keys, values, allowed)

    def total(r):
        result = None
        for piece in range(PIECES):
            block = from_left[piece][0]
            if r > 0:
                block = jnp.where(plane >= r, from_left[piece][r], from_right[piece][ring - r])
            out_rows = output_tiles[piece * step : (piece + 1) * step]
            product = jnp.dot(block, out_rows, preferred_element_type=jnp.float32)
            result = product if result is None else result + product
        return result.reshape(4, owned, depth)

    def outgoing(four):
        return jnp.stack([four[1], four[3]]).astype(jnp.bfloat16)

    def over_core(four, away):
        landed = partner_2(away, "mp", 0).astype(jnp.float32)
        return four[0] + landed[0], (four[2] + landed[1]).astype(jnp.bfloat16)

    def over_y(near, far):
        return (near + partner_2(far, "mp", 1).astype(jnp.float32)).astype(jnp.bfloat16)

    arrived, finished = {}, {}
    attended = (ring - 1) * PIECES + 1
    from_left = [[] for _ in range(PIECES)]
    from_right = [[] for _ in range(PIECES)]
    hops = ring - 1
    for tick in range(1, hops * PIECES + 2 + hops):
        payloads, receivers = [], []
        attending = None
        extra = []
        if tick == 1:
            extra = [blocks[2]]
        elif tick == attended + 1:
            first_four = total(0)
            extra = [outgoing(first_four)]
            for piece in range(PIECES - 1):
                extra += [from_left[piece][hops], from_right[piece][hops]]
        elif tick == attended + 2:
            extra = [far]
        elif tick == attended + 3:
            middle_four = total(2)
            extra = [outgoing(middle_four)]
        for piece in range(PIECES):
            k = tick - hops * piece
            if 1 <= k <= hops:
                going_right, going_left = part(piece, k), part(piece, ring - k)
                if k > 1:
                    going_right += arrived[piece][0].astype(jnp.float32)
                    going_left += arrived[piece][1].astype(jnp.float32)
                payloads += [going_right.astype(jnp.bfloat16), going_left.astype(jnp.bfloat16)]
                receivers.append(("sum", piece, k))
            if k == ring:
                own = part(piece, 0)
                for value in arrived[piece]:
                    own += value.astype(jnp.float32)
                attending = piece
                payloads.insert(0, own)
            k = k - ring
            if 1 <= k <= hops:
                payloads += [from_left[piece][-1], from_right[piece][-1]]
                receivers.append(("gather", piece, k))
        payloads = list(lax.optimization_barrier(tuple(extra + payloads)))
        extra, payloads = payloads[: len(extra)], payloads[len(extra) :]
        if tick == 1:
            slots[2] = beside(extra[0])
        elif tick == attended + 1:
            near, far = over_core(first_four, extra[0])
            for piece in range(PIECES - 1):
                from_left[piece][hops], from_right[piece][hops] = extra[
                    2 * piece + 1 : 2 * piece + 3
                ]
        elif tick == attended + 2:
            finished[0] = over_y(near, extra[0])
        elif tick == attended + 3:
            finished[2] = over_y(*over_core(middle_four, extra[0]))
        if attending is not None:
            own = attend(attending, payloads.pop(0))
            from_left[attending].append(own)
            from_right[attending].append(own)
        for kind, piece, k in receivers:
            first, second = payloads.pop(0), payloads.pop(0)
            if kind == "sum":
                arrived[piece] = hop(first, right[:k]), hop(second, left[hops - k :])
            else:
                from_left[piece].append(hop(first, right[k - 1 :]))
                from_right[piece].append(hop(second, left[: ring - k]))
    out = jnp.zeros((owned, width), jnp.bfloat16)
    for r in (0, 2, 3, 1):
        block = finished.get(r)
        if block is None:
            four = total(r)
            block = over_y(*over_core(four, outgoing(four)))
        if r > 0:
            block = hop(block, [(z, (z - r) % ring) for z in range(ring)])
        out = lax.dynamic_update_slice_in_dim(out, block, (plane + r) % ring * depth, 1)
    return out


def solution(mesh):
    resident = mesh.shape["mp"] == 4 * PART_TIMELINES
    return jax.shard_map(
        resident_weight_shards if resident else gathered_weight_shards,
        mesh=mesh,
        in_specs=(
            P(("group", "mp"), None),
            P(),
            P("mp", None),
            P("mp", None),
            P("mp", None),
            P("mp", None),
            P("group", None),
            P("group"),
        ),
        out_specs=P(("group", "mp"), None),
        check_vma=False,
    )
```
